32 devices in a mesh: pipe: 4 (over y, x), seq: 8 (over z, core).
Axes of the slice: x: 2, y: 2, z: 4, core: 2. Of those that a mesh axis runs over, the one named last changes fastest.
Arguments:
- in_flight: bfloat16 [4, 8192, 1024], P('pipe', 'seq'), may hold values from -6 to 6
- fresh_rows: bfloat16 [8192, 1024], P('seq'), may hold values from -6 to 6
- right_factor: bfloat16 [4, 32, 256, 256], P('pipe', 'seq'), may hold values from -0.375 to 0.375
- left_factor: bfloat16 [4, 256, 32, 32], P('pipe', 'seq'), may hold values from -1 to 1
- gate_gain: float32 [4, 1024], P('pipe'), may hold values from -4 to 4
- gate_bias: float32 [4, 1024], P('pipe'), may hold values from -4 to 4
- norm_gain: float32 [4, 1024], P('pipe'), may hold values from 0.5 to 1.5
- w_up: bfloat16 [4, 4, 256, 512], P('pipe'), may hold values from -0.375 to 0.375
- w_down: bfloat16 [4, 4, 4, 128, 256], P('pipe'), may hold values from -0.25 to 0.25
Outputs:
- first_tick: bfloat16 [4, 8192, 1024], P('pipe', 'seq')
- second_tick: bfloat16 [4, 8192, 1024], P('pipe', 'seq')
The draws below stay inside these ranges and needn't reach their ends.
All inputs are finite; a program needn't handle non-finite values.
Results may differ from the reference program's by a relative error of at most 0.007.
Values may be sent and summed in bfloat16 or wider, within the bound.
A program may use at most 128 MiB of HBM per device.

```python
import jax
import jax.numpy as jnp
from jax import lax

D = 1024
NB = 4
BLOCK = 256
M = 32
SEQ = 8192
LAYERS = 4
DB = 256
FB = 512
Q = 128


def block_levels(key, extent, shards, smallest, high):
    loudness, own = 1.0, jax.random.fold_in(key, 6)
    for dim, shards_of in shards:
        draws = jnp.exp(jax.random.uniform(jax.random.fold_in(own, dim), (shards_of,), jnp.float32, smallest / len(shards), high / len(shards)))
        loudness = loudness * jnp.repeat(draws, extent[dim] // shards_of).reshape([-1 if axis == dim else 1 for axis in range(len(extent))])
    return loudness


def scatter_about(stream_key, extent, spread, bound, shards=(), kind=jnp.bfloat16):
    values = spread * jax.random.normal(stream_key, extent, jnp.float32)
    if shards:
        values = values * block_levels(stream_key, extent, shards, -0.22, 0.18)
    return jnp.clip(values, -bound, bound).astype(kind)


def setup_inputs(seed: int = 0) -> dict:
    key_of = jax.random.split(jax.random.key(seed), 10)
    in_flight = scatter_about(key_of[0], (LAYERS, SEQ, D), 1.0, 6.0, ((0, 4), (1, 8)))
    fresh_rows = scatter_about(key_of[1], (SEQ, D), 1.0, 6.0, ((0, 8),))
    right_factor = scatter_about(key_of[2], (LAYERS, M, BLOCK, BLOCK), BLOCK ** -0.5, 0.375, ((0, 4), (1, 8)))
    left_factor = scatter_about(key_of[3], (LAYERS, BLOCK, M, M), M ** -0.5, 1.0, ((0, 4), (1, 8)))
    gate_gain = scatter_about(key_of[4], (LAYERS, D), 1.0, 4.0, ((0, 4),), jnp.float32)
    gate_bias = scatter_about(key_of[5], (LAYERS, D), 1.0, 4.0, ((0, 4),), jnp.float32)
    norm_gain = jnp.clip(0.5 + 1.0 * jax.random.uniform(key_of[6], (LAYERS, D), jnp.float32) ** block_levels(key_of[6], (LAYERS, D), ((0, 4),), -0.2, 0.2), 0.5, 1.5)
    w_up = scatter_about(key_of[7], (LAYERS, NB, DB, FB), DB ** -0.5, 0.375, ((0, 4),))
    w_down = scatter_about(key_of[8], (LAYERS, NB, NB, Q, DB), FB ** -0.5, 0.25, ((0, 4),))
    return dict(in_flight=in_flight, fresh_rows=fresh_rows, right_factor=right_factor, left_factor=left_factor, gate_gain=gate_gain, gate_bias=gate_bias, norm_gain=norm_gain, w_up=w_up, w_down=w_down)


def one_layer(rows, right_blocks, left_blocks, gate_slope, gate_shift, gain, up_weight, down_weight):
    blocked = rows.reshape(M, BLOCK, D).astype(jnp.float32)
    first_mix = jnp.einsum('ikj,ijc->ikc', right_blocks.astype(jnp.float32), blocked).astype(jnp.bfloat16)
    second_mix = jnp.einsum('jpi,ijc->pjc', left_blocks.astype(jnp.float32), first_mix.astype(jnp.float32)).astype(jnp.bfloat16)
    mixed_seq = second_mix.reshape(M * BLOCK, D).astype(jnp.float32)
    input_wide = rows.astype(jnp.float32)
    residual = input_wide + mixed_seq * jax.nn.sigmoid(input_wide * gate_slope + gate_shift)
    scale_row = lax.rsqrt(lax.optimization_barrier(jnp.mean(residual * residual, axis=-1, keepdims=True)) + 1e-06)
    normed = (residual * scale_row * gain).astype(jnp.bfloat16)
    up_proj = jnp.einsum('tbd,bdf->tbf', normed.reshape(-1, NB, DB).astype(jnp.float32), up_weight.astype(jnp.float32))
    hidden = jax.nn.gelu(up_proj, approximate=True).astype(jnp.bfloat16)
    down_proj = jnp.einsum('tbkq,kbqe->tke', hidden.reshape(-1, NB, NB, Q).astype(jnp.float32), down_weight.astype(jnp.float32))
    return (residual + down_proj.reshape(-1, D)).astype(jnp.bfloat16)

def apply_layer(layer, rows, right_factor, left_factor, gate_gain, gate_bias, norm_gain, w_up, w_down):
    return one_layer(rows, right_factor[layer], left_factor[layer], gate_gain[layer], gate_bias[layer], norm_gain[layer], w_up[layer], w_down[layer])

def reference(in_flight, fresh_rows, right_factor, left_factor, gate_gain, gate_bias, norm_gain, w_up, w_down):
    first_list = []
    for layer in range(LAYERS):
        first_list.append(apply_layer(layer, in_flight[layer], right_factor, left_factor, gate_gain, gate_bias, norm_gain, w_up, w_down))
    second_list = []
    for layer in range(LAYERS):
        source = fresh_rows if layer == 0 else first_list[layer - 1]
        second_list.append(apply_layer(layer, source, right_factor, left_factor, gate_gain, gate_bias, norm_gain, w_up, w_down))
    return (jnp.stack(first_list, axis=0), jnp.stack(second_list, axis=0))
```

```python
import functools

import jax
import jax.numpy as jnp
from jax import lax
from jax.experimental import pallas as pl
from jax.experimental.pallas import tpu as pltpu
from jax.sharding import PartitionSpec as P

BLOCK = 256
GROUP = 16
VMEM_LIMIT = 56 * 1024 * 1024
MESH = pl.DeviceIdType.MESH


def shifted(block, axis, distance):
    devices = range(lax.axis_size(axis))
    route = [(i - distance, i) for i in devices if i - distance in devices]
    return lax.ppermute(block, axis, route)


def channel_part(rows, returned, gate_slope, gate_shift, gain, up_weight, down_weight):
    input_wide = rows.astype(jnp.float32)
    mixed_seq = returned.reshape(rows.shape).astype(jnp.float32)
    residual = input_wide + mixed_seq * jax.nn.sigmoid(input_wide * gate_slope + gate_shift)
    scale_row = lax.rsqrt(jnp.mean(residual * residual, axis=-1, keepdims=True) + 1e-06)
    normed = (residual * scale_row * gain).astype(jnp.bfloat16)
    blocks_count = up_weight.shape[0]
    up_proj = jnp.einsum(
        "tbd,bdf->tbf",
        normed.reshape(rows.shape[0], blocks_count, -1),
        up_weight,
        preferred_element_type=jnp.float32,
    )
    hidden = jax.nn.gelu(up_proj, approximate=True).astype(jnp.bfloat16)
    hidden = hidden.reshape(rows.shape[0], blocks_count, blocks_count, down_weight.shape[2])
    down_proj = jnp.einsum(
        "tbkq,kbqe->tke", hidden, down_weight, preferred_element_type=jnp.float32
    )
    return (residual + down_proj.reshape(rows.shape)).astype(jnp.bfloat16)


def one_layer(
    rows, right_blocks, left_blocks, gate_slope, gate_shift, gain, up_weight, down_weight
):
    tok_rows, width = rows.shape
    blocks_here = right_blocks.shape[0]
    seq_devices = lax.axis_size("seq")
    cols_here = left_blocks.shape[0]
    blocked = rows.reshape(blocks_here, BLOCK, width)
    first_mix = jnp.einsum(
        "ikj,ijc->ikc", right_blocks, blocked, preferred_element_type=jnp.float32
    ).astype(jnp.bfloat16)
    grouped = first_mix.reshape(blocks_here, seq_devices, cols_here, width)
    arrived = lax.all_to_all(grouped, "seq", split_axis=1, concat_axis=0, tiled=True)
    second_mix = jnp.einsum(
        "jpi,ijc->pjc", left_blocks, arrived[:, 0], preferred_element_type=jnp.float32
    ).astype(jnp.bfloat16)
    regrouped = second_mix.reshape(seq_devices, blocks_here, cols_here, width)
    returned = lax.all_to_all(regrouped, "seq", split_axis=0, concat_axis=2, tiled=True)
    return channel_part(rows, returned, gate_slope, gate_shift, gain, up_weight, down_weight)


def shards(
    in_flight, fresh_rows, right_factor, left_factor, gate_gain, gate_bias, norm_gain, w_up, w_down
):
    segment_index = lax.axis_index("pipe")
    weights = (
        right_factor[0],
        left_factor[0],
        gate_gain[0],
        gate_bias[0],
        norm_gain[0],
        w_up[0],
        w_down[0],
    )
    first_out = one_layer(in_flight[0], *weights)
    received = shifted(first_out, "pipe", 1)
    current = jnp.where(segment_index == 0, fresh_rows, received)
    second_out = one_layer(current, *weights)
    return (first_out[None], second_out[None])


def relay_kernel(
    sections, peers,
    rows_ref, fresh_ref, right_ref, left_ref, slope_ref, shift_ref, gain_ref, up_ref, down_ref,
    first_ref, second_ref,
    mixed, arrived, spread, returned, relayed, expanded, hidden, residuals,
    send_sem, recv_sem, relay_send, relay_recv,
):
    here = lax.axis_index("seq")
    section = lax.axis_index("pipe")
    blocks_here, block, width = rows_ref.shape
    cols = block // peers
    half = peers // 2
    offsets = sorted(range(1, peers), key=lambda d: abs(d - half))

    def partner(offset):
        return lax.rem(here + offset, peers)

    def own_rows(device):
        return pl.ds(pl.multiple_of(device * cols, cols), cols)

    barrier = pltpu.get_barrier_semaphore()
    for offset in offsets:
        pl.semaphore_signal(
            barrier, inc=1, device_id=(section, partner(offset)), device_id_type=MESH
        )

    for other in (section + 1, section + sections - 1):
        pl.semaphore_signal(
            barrier, inc=1, device_id=(lax.rem(other, sections), here), device_id_type=MESH
        )
    pl.semaphore_wait(barrier, peers + 1)

    def out_copy(tick, b, device, owner):
        return pltpu.make_async_remote_copy(
            src_ref=mixed.at[tick, b, own_rows(device)],
            dst_ref=arrived.at[tick, owner * blocks_here + b],
            send_sem=send_sem.at[tick, 0, b, device],
            recv_sem=recv_sem.at[tick, 0, b, owner],
            device_id=(section, device),
            device_id_type=MESH,
        )

    def back_copy(tick, b, device, owner):
        return pltpu.make_async_remote_copy(
            src_ref=spread.at[tick, device * blocks_here + b],
            dst_ref=returned.at[tick, b, own_rows(owner)],
            send_sem=send_sem.at[tick, 1, b, device],
            recv_sem=recv_sem.at[tick, 1, b, owner],
            device_id=(section, device),
            device_id_type=MESH,
        )

    def relay_copy(b):
        return pltpu.make_async_remote_copy(
            src_ref=first_ref.at[b],
            dst_ref=relayed.at[b],
            send_sem=relay_send.at[b],
            recv_sem=relay_recv.at[b],
            device_id=(lax.rem(section + 1, sections), here),
            device_id_type=MESH,
        )

    def first_factor(tick, b, source):
        mixed[tick, b] = jnp.dot(
            right_ref[b], source[b], preferred_element_type=jnp.float32
        ).astype(jnp.bfloat16)
        for offset in offsets:
            out_copy(tick, b, partner(offset), here).start()
        arrived[tick, here * blocks_here + b] = mixed[tick, b, own_rows(here)]

    def second_factor(tick):
        def wait_block(b, carry):
            for offset in offsets:
                out_copy(tick, b, here, partner(offset)).wait_recv()
            return carry

        lax.fori_loop(0, blocks_here, wait_block, 0)
        piece = width // 2
        for g in range(cols // GROUP):
            band = slice(g * GROUP, (g + 1) * GROUP)
            for c in range(0, width, piece):
                taken = arrived[tick, :, band, c : c + piece].reshape(-1, piece)
                product = jnp.dot(expanded[g], taken, preferred_element_type=jnp.float32)
                spread[tick, :, band, c : c + piece] = product.astype(jnp.bfloat16).reshape(
                    -1, GROUP, piece
                )

        def send_block(b, carry):
            for offset in offsets:
                back_copy(tick, b, partner(offset), here).start()
            returned[tick, b, own_rows(here)] = spread[tick, here * blocks_here + b]
            return carry

        lax.fori_loop(0, blocks_here, send_block, 0)

    def channel_block(tick, b, source, target):
        for offset in offsets:
            back_copy(tick, b, here, partner(offset)).wait_recv()
        wide = source[b].astype(jnp.float32)
        gate = jax.nn.sigmoid(wide * slope_ref[...] + shift_ref[...])
        residual = wide + returned[tick, b].astype(jnp.float32) * gate
        residuals[...] = residual
        scale = lax.rsqrt(jnp.mean(residual * residual, axis=-1, keepdims=True) + 1e-06)
        parts = up_ref.shape[0]
        step = width // parts
        q = up_ref.shape[2] // parts
        for p in range(parts):
            band = slice(p * step, (p + 1) * step)
            normed = (residuals[:, band] * scale * gain_ref[:, band]).astype(jnp.bfloat16)
            up = jnp.dot(normed, up_ref[p], preferred_element_type=jnp.float32)
            act = jax.nn.gelu(up, approximate=True).astype(jnp.bfloat16)
            for k in range(parts):
                hidden[k, :, p * q : (p + 1) * q] = act[:, k * q : (k + 1) * q]
        for k in range(parts):
            band = slice(k * step, (k + 1) * step)
            down = jnp.dot(hidden[k], down_ref[k], preferred_element_type=jnp.float32)
            target[b, :, band] = (residuals[:, band] + down).astype(jnp.bfloat16)

    def opening(b, carry):
        first_factor(0, b, rows_ref)
        return carry

    lax.fori_loop(0, blocks_here, opening, 0)

    total = left_ref.shape[2]
    size = total * GROUP
    picks = lax.broadcasted_iota(jnp.int32, (total, size), 1) // GROUP
    repeat = (picks == lax.broadcasted_iota(jnp.int32, (total, size), 0)).astype(jnp.bfloat16)
    same = lax.rem(lax.broadcasted_iota(jnp.int32, (size, size), 0), GROUP) == lax.rem(
        lax.broadcasted_iota(jnp.int32, (size, size), 1), GROUP
    )
    for g in range(cols // GROUP):
        repeated = jnp.dot(left_ref[g], repeat, preferred_element_type=jnp.float32)
        expanded[g] = jnp.where(same, repeated, 0.0).astype(jnp.bfloat16)

    @pl.when(section == 0)
    def _():
        relayed[...] = fresh_ref[...]

    second_factor(0)

    def enter(b):
        @pl.when(section > 0)
        def _():
            relay_copy(b).wait_recv()

        first_factor(1, b, relayed)

    def middle(b, carry):
        channel_block(0, b, rows_ref, first_ref)

        @pl.when(section < sections - 1)
        def _():
            relay_copy(b).start()

        @pl.when(b > 0)
        def _():
            enter(b - 1)

        return carry

    lax.fori_loop(0, blocks_here, middle, 0)
    enter(blocks_here - 1)
    second_factor(1)

    def closing(b, carry):
        channel_block(1, b, relayed, second_ref)
        return carry

    lax.fori_loop(0, blocks_here, closing, 0)

    def drain(b, carry):
        for offset in offsets:
            for tick in range(2):
                out_copy(tick, b, partner(offset), here).wait_send()
                back_copy(tick, b, partner(offset), here).wait_send()

        @pl.when(section < sections - 1)
        def _():
            relay_copy(b).wait_send()

        return carry

    lax.fori_loop(0, blocks_here, drain, 0)


def relay_shards(
    in_flight, fresh_rows, right_factor, left_factor, gate_gain, gate_bias, norm_gain, w_up, w_down
):
    sections, peers = lax.axis_size("pipe"), lax.axis_size("seq")
    blocks_here = right_factor.shape[1]
    cols, total = left_factor.shape[1:3]
    width = fresh_rows.shape[1]
    groups = cols // GROUP
    blocked = (blocks_here, BLOCK, width)
    parts, step, wide = w_up.shape[1:]
    left = left_factor[0].reshape(groups, GROUP, total, total).transpose(0, 2, 1, 3)
    left = left.reshape(groups, total * GROUP, total)
    whole = pl.BlockSpec(memory_space=pltpu.VMEM)
    bf16 = jnp.bfloat16
    first, second = pl.pallas_call(
        functools.partial(relay_kernel, sections, peers),
        out_shape=[jax.ShapeDtypeStruct(blocked, bf16)] * 2,
        in_specs=[whole] * 9,
        out_specs=[whole] * 2,
        scratch_shapes=[
            pltpu.VMEM((2, blocks_here, BLOCK, width), bf16),
            pltpu.VMEM((2, total, cols, width), bf16),
            pltpu.VMEM((2, total, cols, width), bf16),
            pltpu.VMEM((2, blocks_here, BLOCK, width), bf16),
            pltpu.VMEM(blocked, bf16),
            pltpu.VMEM((groups, total * GROUP, total * GROUP), bf16),
            pltpu.VMEM((parts, BLOCK, wide), bf16),
            pltpu.VMEM((BLOCK, width), jnp.float32),
            pltpu.SemaphoreType.DMA((2, 2, blocks_here, peers)),
            pltpu.SemaphoreType.DMA((2, 2, blocks_here, peers)),
            pltpu.SemaphoreType.DMA((blocks_here,)),
            pltpu.SemaphoreType.DMA((blocks_here,)),
        ],
        compiler_params=pltpu.CompilerParams(
            collective_id=0, has_side_effects=True, vmem_limit_bytes=VMEM_LIMIT
        ),
    )(
        in_flight.reshape(blocked),
        fresh_rows.reshape(blocked),
        right_factor[0],
        left,
        gate_gain,
        gate_bias,
        norm_gain,
        w_up[0],
        w_down.reshape(parts, wide, step),
    )
    return first.reshape(in_flight.shape), second.reshape(in_flight.shape)


def solution(mesh):
    peers = mesh.shape["seq"]
    body = relay_shards if BLOCK % (peers * GROUP) == 0 else shards
    in_specs = (
        P("pipe", "seq", None),
        P("seq", None),
        P("pipe", "seq", None, None),
        P("pipe", "seq", None, None),
        P("pipe", None),
        P("pipe", None),
        P("pipe", None),
        P("pipe", None, None, None),
        P("pipe", None, None, None, None),
    )
    out_specs = (P("pipe", "seq", None), P("pipe", "seq", None))
    return jax.shard_map(body, mesh=mesh, in_specs=in_specs, out_specs=out_specs, check_vma=False)
```

```python
import functools

import jax
import jax.numpy as jnp
from jax import lax
from jax.experimental import pallas as pl
from jax.experimental.pallas import tpu as pltpu
from jax.sharding import PartitionSpec as P

BLOCK = 256
GROUP = 16
VMEM_LIMIT = 56 * 1024 * 1024
MESH = pl.DeviceIdType.MESH


def shifted(block, axis, distance):
    devices = range(lax.axis_size(axis))
    route = [(i - distance, i) for i in devices if i - distance in devices]
    return lax.ppermute(block, axis, route)


def channel_part(rows, returned, gate_slope, gate_shift, gain, up_weight, down_weight):
    input_wide = rows.astype(jnp.float32)
    mixed_seq = returned.reshape(rows.shape).astype(jnp.float32)
    residual = input_wide + mixed_seq * jax.nn.sigmoid(input_wide * gate_slope + gate_shift)
    scale_row = lax.rsqrt(jnp.mean(residual * residual, axis=-1, keepdims=True) + 1e-06)
    normed = (residual * scale_row * gain).astype(jnp.bfloat16)
    blocks_count = up_weight.shape[0]
    up_proj = jnp.einsum(
        "tbd,bdf->tbf",
        normed.reshape(rows.shape[0], blocks_count, -1),
        up_weight,
        preferred_element_type=jnp.float32,
    )
    hidden = jax.nn.gelu(up_proj, approximate=True).astype(jnp.bfloat16)
    hidden = hidden.reshape(rows.shape[0], blocks_count, blocks_count, down_weight.shape[2])
    down_proj = jnp.einsum(
        "tbkq,kbqe->tke", hidden, down_weight, preferred_element_type=jnp.float32
    )
    return (residual + down_proj.reshape(rows.shape)).astype(jnp.bfloat16)


def one_layer(
    rows, right_blocks, left_blocks, gate_slope, gate_shift, gain, up_weight, down_weight
):
    tok_rows, width = rows.shape
    blocks_here = right_blocks.shape[0]
    seq_devices = lax.axis_size("seq")
    cols_here = left_blocks.shape[0]
    blocked = rows.reshape(blocks_here, BLOCK, width)
    first_mix = jnp.einsum(
        "ikj,ijc->ikc", right_blocks, blocked, preferred_element_type=jnp.float32
    ).astype(jnp.bfloat16)
    grouped = first_mix.reshape(blocks_here, seq_devices, cols_here, width)
    arrived = lax.all_to_all(grouped, "seq", split_axis=1, concat_axis=0, tiled=True)
    second_mix = jnp.einsum(
        "jpi,ijc->pjc", left_blocks, arrived[:, 0], preferred_element_type=jnp.float32
    ).astype(jnp.bfloat16)
    regrouped = second_mix.reshape(seq_devices, blocks_here, cols_here, width)
    returned = lax.all_to_all(regrouped, "seq", split_axis=0, concat_axis=2, tiled=True)
    return channel_part(rows, returned, gate_slope, gate_shift, gain, up_weight, down_weight)


def shards(
    in_flight, fresh_rows, right_factor, left_factor, gate_gain, gate_bias, norm_gain, w_up, w_down
):
    segment_index = lax.axis_index("pipe")
    weights = (
        right_factor[0],
        left_factor[0],
        gate_gain[0],
        gate_bias[0],
        norm_gain[0],
        w_up[0],
        w_down[0],
    )
    first_out = one_layer(in_flight[0], *weights)
    received = shifted(first_out, "pipe", 1)
    current = jnp.where(segment_index == 0, fresh_rows, received)
    second_out = one_layer(current, *weights)
    return (first_out[None], second_out[None])


def relay_kernel(
    sections, peers,
    rows_hbm, fresh_hbm, right_hbm, left_hbm, slope_ref, shift_ref, gain_ref, up_hbm, down_hbm,
    first_hbm, second_hbm,
    rows_ref, right_ref, left_ref, up_ref, down_ref, first_ref, second_ref,
    mixed, arrived, spread, returned, relayed, expanded, hidden, residuals,
    send_sem, recv_sem, relay_send, relay_recv, load_sem, weight_sem, fresh_sem, store_sem,
):
    here = lax.axis_index("seq")
    section = lax.axis_index("pipe")
    blocks_here, block, width = rows_ref.shape
    cols = block // peers
    half = peers // 2
    groups = cols // GROUP
    last = blocks_here - 1
    offsets = sorted(range(1, peers), key=lambda d: abs(d - half))

    def partner(offset):
        return lax.rem(here + offset, peers)

    def own_rows(device):
        return pl.ds(pl.multiple_of(device * cols, cols), cols)

    def load_rows(b):
        return pltpu.make_async_copy(rows_hbm.at[b], rows_ref.at[b], load_sem.at[0, b])

    def load_right(b):
        return pltpu.make_async_copy(right_hbm.at[b], right_ref.at[b], load_sem.at[1, b])

    load_left = pltpu.make_async_copy(left_hbm, left_ref, weight_sem.at[0])
    load_up = pltpu.make_async_copy(up_hbm, up_ref, weight_sem.at[1])
    load_down = pltpu.make_async_copy(down_hbm, down_ref, weight_sem.at[2])
    load_fresh = pltpu.make_async_copy(fresh_hbm, relayed, fresh_sem)

    def store(tick, b):
        source, target = ((first_ref, first_hbm), (second_ref, second_hbm))[tick]
        return pltpu.make_async_copy(source.at[b], target.at[b], store_sem.at[tick, b])

    for b in range(blocks_here):
        load_right(b).start()
        load_rows(b).start()

    barrier = pltpu.get_barrier_semaphore()
    for offset in offsets:
        pl.semaphore_signal(
            barrier, inc=1, device_id=(section, partner(offset)), device_id_type=MESH
        )

    for other in (section + 1, section + sections - 1):
        pl.semaphore_signal(
            barrier, inc=1, device_id=(lax.rem(other, sections), here), device_id_type=MESH
        )
    pl.semaphore_wait(barrier, peers + 1)

    def out_copy(tick, b, device, owner, piece=None):
        start, count = (0, cols) if piece is None else (piece * GROUP, GROUP)
        slot = b if piece is None else last + piece
        rows = pl.ds(pl.multiple_of(device * cols + start, count), count)
        return pltpu.make_async_remote_copy(
            src_ref=mixed.at[tick, b, rows],
            dst_ref=arrived.at[tick, owner * blocks_here + b, pl.ds(start, count)],
            send_sem=send_sem.at[tick, 0, slot, device],
            recv_sem=recv_sem.at[tick, 0, slot, owner],
            device_id=(section, device),
            device_id_type=MESH,
        )

    def back_copy(tick, b, device, owner, piece=None):
        start, count = (0, cols) if piece is None else (piece * GROUP, GROUP)
        slot = groups - 1 + b if piece is None else piece
        rows = pl.ds(pl.multiple_of(owner * cols + start, count), count)
        return pltpu.make_async_remote_copy(
            src_ref=spread.at[tick, device * blocks_here + b, pl.ds(start, count)],
            dst_ref=returned.at[tick, b, rows],
            send_sem=send_sem.at[tick, 1, slot, device],
            recv_sem=recv_sem.at[tick, 1, slot, owner],
            device_id=(section, device),
            device_id_type=MESH,
        )

    def relay_copy(b):
        return pltpu.make_async_remote_copy(
            src_ref=first_ref.at[b],
            dst_ref=relayed.at[b],
            send_sem=relay_send.at[b],
            recv_sem=relay_recv.at[b],
            device_id=(lax.rem(section + 1, sections), here),
            device_id_type=MESH,
        )

    def first_factor(tick, b, source, pieces=(None,)):
        mixed[tick, b] = jnp.dot(
            right_ref[b], source[b], preferred_element_type=jnp.float32
        ).astype(jnp.bfloat16)
        for piece in pieces:
            for offset in offsets:
                out_copy(tick, b, partner(offset), here, piece).start()
        arrived[tick, here * blocks_here + b] = mixed[tick, b, own_rows(here)]

    def second_factor(tick):
        def wait_block(b, carry):
            for offset in offsets:
                out_copy(tick, b, here, partner(offset)).wait_recv()
            return carry

        lax.fori_loop(0, last, wait_block, 0)
        part = width // 2
        for g in range(groups):
            for offset in offsets:
                out_copy(tick, last, here, partner(offset), g).wait_recv()
            band = slice(g * GROUP, (g + 1) * GROUP)
            for c in range(0, width, part):
                taken = arrived[tick, :, band, c : c + part].reshape(-1, part)
                product = jnp.dot(expanded[g], taken, preferred_element_type=jnp.float32)
                spread[tick, :, band, c : c + part] = product.astype(jnp.bfloat16).reshape(
                    -1, GROUP, part
                )
            for offset in offsets:
                back_copy(tick, 0, partner(offset), here, g).start()

        def send_block(b, carry):
            for offset in offsets:
                back_copy(tick, b, partner(offset), here).start()
            return carry

        lax.fori_loop(1, blocks_here, send_block, 0)

        def keep_block(b, carry):
            returned[tick, b, own_rows(here)] = spread[tick, here * blocks_here + b]
            return carry

        lax.fori_loop(0, blocks_here, keep_block, 0)

    def channel_block(tick, b, source, target):
        @pl.when(b == 0)
        def _():
            for g in range(groups):
                for offset in offsets:
                    back_copy(tick, 0, here, partner(offset), g).wait_recv()

        @pl.when(b > 0)
        def _():
            for offset in offsets:
                back_copy(tick, b, here, partner(offset)).wait_recv()

        wide = source[b].astype(jnp.float32)
        gate = jax.nn.sigmoid(wide * slope_ref[...] + shift_ref[...])
        residual = wide + returned[tick, b].astype(jnp.float32) * gate
        residuals[...] = residual
        scale = lax.rsqrt(jnp.mean(residual * residual, axis=-1, keepdims=True) + 1e-06)
        parts = up_ref.shape[0]
        step = width // parts
        q = up_ref.shape[2] // parts
        for p in range(parts):
            band = slice(p * step, (p + 1) * step)
            normed = (residuals[:, band] * scale * gain_ref[:, band]).astype(jnp.bfloat16)
            up = jnp.dot(normed, up_ref[p], preferred_element_type=jnp.float32)
            act = jax.nn.gelu(up, approximate=True).astype(jnp.bfloat16)
            for k in range(parts):
                hidden[k, :, p * q : (p + 1) * q] = act[:, k * q : (k + 1) * q]
        for k in range(parts):
            band = slice(k * step, (k + 1) * step)
            down = jnp.dot(hidden[k], down_ref[k], preferred_element_type=jnp.float32)
            target[b, :, band] = (residuals[:, band] + down).astype(jnp.bfloat16)
        store(tick, b).start()

    def opening(b, carry):
        load_right(b).wait()
        load_rows(b).wait()
        first_factor(0, b, rows_ref)
        return carry

    lax.fori_loop(0, last, opening, 0)
    load_right(last).wait()
    load_rows(last).wait()
    first_factor(0, last, rows_ref, range(groups))

    load_left.start()
    load_up.start()
    load_down.start()

    @pl.when(section == 0)
    def _():
        load_fresh.start()

    load_left.wait()

    total = left_ref.shape[2]
    size = total * GROUP
    picks = lax.broadcasted_iota(jnp.int32, (total, size), 1) // GROUP
    repeat = (picks == lax.broadcasted_iota(jnp.int32, (total, size), 0)).astype(jnp.bfloat16)
    same = lax.rem(lax.broadcasted_iota(jnp.int32, (size, size), 0), GROUP) == lax.rem(
        lax.broadcasted_iota(jnp.int32, (size, size), 1), GROUP
    )
    into = lax.broadcasted_iota(jnp.int32, (size, size), 0)
    swap = lax.rem(into, GROUP) * total + into // GROUP
    swap = (swap == lax.broadcasted_iota(jnp.int32, (size, size), 1)).astype(jnp.bfloat16)
    for g in range(groups):
        swapped = jnp.dot(swap, left_ref[g], preferred_element_type=jnp.float32)
        repeated = jnp.dot(
            swapped.astype(jnp.bfloat16), repeat, preferred_element_type=jnp.float32
        )
        expanded[g] = jnp.where(same, repeated, 0.0).astype(jnp.bfloat16)

    load_up.wait()
    load_down.wait()

    @pl.when(section == 0)
    def _():
        load_fresh.wait()

    second_factor(0)

    def enter(b, pieces=(None,)):
        @pl.when(section > 0)
        def _():
            relay_copy(b).wait_recv()

        first_factor(1, b, relayed, pieces)

    def middle(b, carry):
        channel_block(0, b, rows_ref, first_ref)

        @pl.when(section < sections - 1)
        def _():
            relay_copy(b).start()

        @pl.when(b > 0)
        def _():
            enter(b - 1)

        return carry

    lax.fori_loop(0, blocks_here, middle, 0)
    enter(last, range(groups))
    second_factor(1)

    def closing(b, carry):
        channel_block(1, b, relayed, second_ref)
        return carry

    lax.fori_loop(0, blocks_here, closing, 0)

    def drain(b, carry):
        for offset in offsets:
            for tick in range(2):
                out_copy(tick, b, partner(offset), here).wait_send()
                back_copy(tick, b + 1, partner(offset), here).wait_send()
        return carry

    lax.fori_loop(0, last, drain, 0)
    for offset in offsets:
        for tick in range(2):
            for g in range(groups):
                out_copy(tick, last, partner(offset), here, g).wait_send()
                back_copy(tick, 0, partner(offset), here, g).wait_send()

    @pl.when(section < sections - 1)
    def _():
        for b in range(blocks_here):
            relay_copy(b).wait_send()

    for tick in range(2):
        for b in range(blocks_here):
            store(tick, b).wait()


def relay_shards(
    in_flight, fresh_rows, right_factor, left_factor, gate_gain, gate_bias, norm_gain, w_up, w_down
):
    sections, peers = lax.axis_size("pipe"), lax.axis_size("seq")
    blocks_here = right_factor.shape[1]
    cols, total = left_factor.shape[1:3]
    width = fresh_rows.shape[1]
    groups = cols // GROUP
    blocked = (blocks_here, BLOCK, width)
    parts, step, wide = w_up.shape[1:]
    left = left_factor.reshape(groups, GROUP * total, total)
    whole = pl.BlockSpec(memory_space=pltpu.VMEM)
    far = pl.BlockSpec(memory_space=pl.ANY)
    slots = blocks_here - 1 + groups
    bf16 = jnp.bfloat16
    first, second = pl.pallas_call(
        functools.partial(relay_kernel, sections, peers),
        out_shape=[jax.ShapeDtypeStruct(blocked, bf16)] * 2,
        in_specs=[far] * 4 + [whole] * 3 + [far] * 2,
        out_specs=[far] * 2,
        scratch_shapes=[
            pltpu.VMEM(blocked, bf16),
            pltpu.VMEM((blocks_here, BLOCK, BLOCK), bf16),
            pltpu.VMEM(left.shape, bf16),
            pltpu.VMEM((parts, step, wide), bf16),
            pltpu.VMEM((parts, wide, step), bf16),
            pltpu.VMEM(blocked, bf16),
            pltpu.VMEM(blocked, bf16),
            pltpu.VMEM((2, blocks_here, BLOCK, width), bf16),
            pltpu.VMEM((2, total, cols, width), bf16),
            pltpu.VMEM((2, total, cols, width), bf16),
            pltpu.VMEM((2, blocks_here, BLOCK, width), bf16),
            pltpu.VMEM(blocked, bf16),
            pltpu.VMEM((groups, total * GROUP, total * GROUP), bf16),
            pltpu.VMEM((parts, BLOCK, wide), bf16),
            pltpu.VMEM((BLOCK, width), jnp.float32),
            pltpu.SemaphoreType.DMA((2, 2, slots, peers)),
            pltpu.SemaphoreType.DMA((2, 2, slots, peers)),
            pltpu.SemaphoreType.DMA((blocks_here,)),
            pltpu.SemaphoreType.DMA((blocks_here,)),
            pltpu.SemaphoreType.DMA((2, blocks_here)),
            pltpu.SemaphoreType.DMA((3,)),
            pltpu.SemaphoreType.DMA(()),
            pltpu.SemaphoreType.DMA((2, blocks_here)),
        ],
        compiler_params=pltpu.CompilerParams(
            collective_id=0, has_side_effects=True, vmem_limit_bytes=VMEM_LIMIT
        ),
    )(
        in_flight.reshape(blocked),
        fresh_rows.reshape(blocked),
        right_factor[0],
        left,
        gate_gain,
        gate_bias,
        norm_gain,
        w_up[0],
        w_down.reshape(parts, wide, step),
    )
    return first.reshape(in_flight.shape), second.reshape(in_flight.shape)


def solution(mesh):
    peers = mesh.shape["seq"]
    body = relay_shards if BLOCK % (peers * GROUP) == 0 else shards
    in_specs = (
        P("pipe", "seq", None),
        P("seq", None),
        P("pipe", "seq", None, None),
        P("pipe", "seq", None, None),
        P("pipe", None),
        P("pipe", None),
        P("pipe", None),
        P("pipe", None, None, None),
        P("pipe", None, None, None, None),
    )
    out_specs = (P("pipe", "seq", None), P("pipe", "seq", None))
    return jax.shard_map(body, mesh=mesh, in_specs=in_specs, out_specs=out_specs, check_vma=False)
```
